256 devices in a mesh: row: 32 (over x, y, core), col: 8 (over z).
Axes of the slice: x: 4, y: 4, z: 8, core: 2. Of those that a mesh axis runs over, the one named last changes fastest.
Arguments:
- inputs: bfloat16 [768, 12288], P('row', 'col'), may hold values from -6 to 6
- w_in: bfloat16 [12288, 24576], P('col', 'row'), may hold values from -0.0546875 to 0.0546875
- w_out: bfloat16 [24576, 12288], P('row', 'col'), may hold values from -0.0390625 to 0.0390625
- out_grad: bfloat16 [768, 12288], P('row', 'col'), may hold values from -6 to 6
Outputs:
- output: bfloat16 [768, 12288], P('row', 'col')
- input_grad: bfloat16 [768, 12288], P('row', 'col')
- grad_in_w: bfloat16 [12288, 24576], P('col', 'row')
- grad_out_w: bfloat16 [24576, 12288], P('row', 'col')
The draws below stay inside these ranges and needn't reach their ends.
All inputs are finite; a program needn't handle non-finite values.
Results may differ from the reference program's by a relative error of at most 0.0049.
Values may be sent and summed in bfloat16 or wider, within the bound.
No kernel may reach another device: no remote copies, remote signals or barrier semaphores. Data moves between devices by JAX's collectives and lax.ppermute only.
A program may use at most 128 MiB of HBM per device.

```python
import jax
import jax.numpy as jnp
from jax import lax

D = 12288
FF = 24576
TOKENS = 768


def block_scale(key, shape, split, low, high):
    def one(axis_at, shards_of):
        heights = jax.random.uniform(jax.random.fold_in(jax.random.fold_in(key, 6), axis_at), (shards_of,), jnp.float32, low / len(split), high / len(split))
        return jnp.repeat(jnp.exp(heights), shape[axis_at] // shards_of).reshape((-1,) + (1,) * (len(shape) - axis_at - 1))

    factor_of = one(*split[0])
    for cut in split[1:]:
        factor_of = factor_of * one(*cut)
    return factor_of


def gaussian(key, shape, scale, reach, cuts=(), kind=jnp.bfloat16):
    drawn = scale * jax.random.normal(key, shape, jnp.float32)
    if cuts:
        drawn = drawn * block_scale(key, shape, cuts, -0.22, 0.18)
    return jnp.clip(drawn, -reach, reach).astype(kind)


def setup_inputs(seed: int = 0) -> dict:
    splits = jax.random.split(jax.random.key(seed), 5)
    return {
        "inputs": gaussian(splits[0], (TOKENS, D), 1.0, 6.0, ((0, 32), (1, 8))),
        "w_in": gaussian(splits[1], (D, FF), D ** -0.5, 0.0546875, ((0, 8), (1, 32))),
        "w_out": gaussian(splits[2], (FF, D), FF ** -0.5, 0.0390625, ((0, 32), (1, 8))),
        "out_grad": gaussian(splits[3], (TOKENS, D), 1.0, 6.0, ((0, 32), (1, 8))),
    }


gelu_scale = 0.7978845608028654
gelu_cubic = 0.044715


def gelu_parts(hidden):
    inner = gelu_scale * (hidden + gelu_cubic * hidden * hidden * hidden)
    tangent = jnp.tanh(inner)
    value = 0.5 * hidden * (1.0 + tangent)
    slopes = 0.5 * (1.0 + tangent) + 0.5 * hidden * (1.0 - tangent * tangent) * gelu_scale * (1.0 + 3.0 * gelu_cubic * hidden * hidden)
    return value, slopes


def contract_first(left, right):
    return lax.dot_general(left, right, (((0,), (0,)), ((), ())), preferred_element_type=jnp.float32)


def contract_last(left, right):
    return lax.dot_general(left, right, (((1,), (1,)), ((), ())), preferred_element_type=jnp.float32)


def reference(inputs, w_in, w_out, out_grad):
    hidden = jnp.dot(inputs, w_in, preferred_element_type=jnp.float32)
    value, slopes = gelu_parts(hidden)
    activation = value.astype(jnp.bfloat16)
    output = jnp.dot(activation, w_out, preferred_element_type=jnp.float32).astype(jnp.bfloat16)
    act_grad = contract_last(out_grad, w_out)
    hid_grad = (act_grad * slopes).astype(jnp.bfloat16)
    grad_out_w = contract_first(activation, out_grad).astype(jnp.bfloat16)
    grad_in_w = contract_first(inputs, hid_grad).astype(jnp.bfloat16)
    input_grad = contract_last(hid_grad, w_in).astype(jnp.bfloat16)
    return output, input_grad, grad_in_w, grad_out_w
```

```python
import functools

import jax
import jax.numpy as jnp
from jax import lax
from jax.experimental import pallas as pl
from jax.experimental.pallas import tpu as pltpu
from jax.sharding import PartitionSpec as P

gelu_scale = 0.7978845608028654
gelu_cubic = 0.044715
f32 = jnp.float32
bf16 = jnp.bfloat16
side = 4
ring = 8
tile = 256
steps = (1, -1, 2)


def gelu_parts(hidden):
    inner = gelu_scale * (hidden + gelu_cubic * hidden * hidden * hidden)
    tangent = jnp.tanh(inner)
    value = 0.5 * hidden * (1.0 + tangent)
    slopes = 0.5 * (1.0 + tangent) + 0.5 * hidden * (1.0 - tangent * tangent) * gelu_scale * (
        1.0 + 3.0 * gelu_cubic * hidden * hidden
    )
    return (value, slopes)


def coded(array):
    array = array * 2.0**30
    return (array * array * array).astype(bf16)


def decoded(array):
    array = array.astype(f32)
    return jnp.sign(array) * jnp.exp2(jnp.log2(jnp.abs(array)) * (1.0 / 3.0) - 30.0)


def place(x, y, core):
    return ((x % side) * side + y % side) * 2 + core


def swap_cores(array):
    return lax.ppermute(
        array, "row", [(place(0, 0, 0) + r, (place(0, 0, 0) + r) ^ 1) for r in range(32)]
    )


def first_axis(array, by):
    pairs = []
    for x in range(side):
        for y in range(side):
            pairs.append((place(x, y, 0), place(x + by, y, 0)))
            pairs.append((place(x, y, 1), place(x, y + by, 1)))
    return lax.ppermute(array, "row", pairs)


def second_axis(array, by):
    pairs = []
    for x in range(side):
        for y in range(side):
            pairs.append((place(x, y, 0), place(x, y + by, 0)))
            pairs.append((place(x, y, 1), place(x + by, y, 1)))
    return lax.ppermute(array, "row", pairs)


def along_z(array, by):
    return lax.ppermute(array, "col", [(z, (z + by) % ring) for z in range(ring)])


def slot(at, outer, inner):
    core, me = at[0], at[1]
    spot = jnp.where(core == 0, inner * side + outer, outer * side + inner)
    return lax.rem(spot // 2 + ring - me, ring), lax.rem(spot, 2)


def first_kernel(at, a0, a1, a2, a3, in_own, in_par, out_own, out_par, h_ref, g_ref, held):
    step = pl.program_id(0)
    core = at[0]

    @pl.when(step == 0)
    def _():
        for outer, ref in enumerate((a0, a1, a2, a3)):
            for inner in range(side):
                chunk, half = slot(at, outer, inner)
                block = ref[pl.ds(inner * 48, 48), :]
                g_ref[chunk, half] = block
                held[chunk, half] = block

    def plain(w):
        a = held[...].reshape(768, 1536)
        h_ref[...] = jnp.dot(a, w[...], preferred_element_type=f32).reshape(h_ref.shape)

    def turned(w):
        a = held[...].reshape(768, 1536)
        h_ref[...] = lax.dot_general(
            a, w[...], (((1,), (1,)), ((), ())), preferred_element_type=f32
        ).reshape(h_ref.shape)

    pl.when((core == 0) & (step < 3))(lambda: plain(in_own))
    pl.when((core == 0) & (step >= 3))(lambda: plain(in_par))
    pl.when((core == 1) & (step < 3))(lambda: turned(out_par))
    pl.when((core == 1) & (step >= 3))(lambda: turned(out_own))


def first_product(at, blocks, in_own, in_par, out_own, out_par):
    whole = pl.BlockSpec((192, 1536), lambda j, at: (0, 0))
    early = lambda j: jnp.minimum(j, 2)
    late = lambda j: jnp.maximum(j - 3, 0)
    return pl.pallas_call(
        first_kernel,
        grid_spec=pltpu.PrefetchScalarGridSpec(
            num_scalar_prefetch=1,
            grid=(6,),
            in_specs=[whole] * 4
            + [
                pl.BlockSpec((1536, tile), lambda j, at: (0, jnp.where(at[0] == 0, early(j), 0))),
                pl.BlockSpec((1536, tile), lambda j, at: (0, jnp.where(at[0] == 0, late(j), 0))),
                pl.BlockSpec((tile, 1536), lambda j, at: (jnp.where(at[0] == 1, late(j), 0), 0)),
                pl.BlockSpec((tile, 1536), lambda j, at: (jnp.where(at[0] == 1, early(j), 0), 0)),
            ],
            out_specs=[
                pl.BlockSpec((ring, 2, 48, tile), lambda j, at: (0, 0, 0, j)),
                pl.BlockSpec((ring, 2, 48, 1536), lambda j, at: (0, 0, 0, 0)),
            ],
            scratch_shapes=[pltpu.VMEM((ring, 2, 48, 1536), bf16)],
        ),
        out_shape=[
            jax.ShapeDtypeStruct((ring, 2, 48, 1536), f32),
            jax.ShapeDtypeStruct((ring, 2, 48, 1536), bf16),
        ],
        compiler_params=pltpu.CompilerParams(vmem_limit_bytes=40 << 20),
        cost_estimate=pl.CostEstimate(
            flops=2 * 768 * 1536 * 1536, bytes_accessed=12 << 20, transcendentals=0
        ),
    )(at, *blocks, in_own, in_par, out_own, out_par)


def second_kernel(at, *refs):
    chunks, (in_own, in_par, out_own, out_par, o_ref, held, made) = refs[:ring], refs[ring:]
    step = pl.program_id(0)
    core, me = at[0], at[1]

    @pl.when(step == 0)
    def _():
        for i, ref in enumerate(chunks):
            held[i] = ref[...]

    def plain(w0, w1):
        b = held[...].reshape(768, 1536)
        made[...] = (
            jnp.dot(b[:, :768], w0[...], preferred_element_type=f32)
            + jnp.dot(b[:, 768:], w1[...], preferred_element_type=f32)
        ).astype(bf16).reshape(made.shape)

    def turned(w0, w1):
        b = held[...].reshape(768, 1536)
        last = (((1,), (1,)), ((), ()))
        made[...] = (
            lax.dot_general(b[:, :768], w0[...], last, preferred_element_type=f32)
            + lax.dot_general(b[:, 768:], w1[...], last, preferred_element_type=f32)
        ).astype(bf16).reshape(made.shape)

    pl.when(core == 0)(lambda: plain(out_own, out_par))
    pl.when(core == 1)(lambda: turned(in_par, in_own))
    for outer in range(side):
        for inner in range(side):
            chunk, half = slot(at, outer, inner)
            o_ref[outer, inner] = made[chunk, half]


def second_product(at, chunks, in_own, in_par, out_own, out_par):
    whole = pl.BlockSpec((96, 1536), lambda j, at: (0, 0))
    on_in = pl.BlockSpec((tile, 768), lambda j, at: (jnp.where(at[0] == 1, j, 0), 0))
    on_out = pl.BlockSpec((768, tile), lambda j, at: (0, jnp.where(at[0] == 0, j, 0)))
    return pl.pallas_call(
        second_kernel,
        grid_spec=pltpu.PrefetchScalarGridSpec(
            num_scalar_prefetch=1,
            grid=(6,),
            in_specs=[whole] * ring + [on_in, on_in, on_out, on_out],
            out_specs=pl.BlockSpec((side, side, 48, tile), lambda j, at: (0, 0, 0, j)),
            scratch_shapes=[
                pltpu.VMEM((ring, 96, 1536), bf16),
                pltpu.VMEM((ring, 2, 48, tile), bf16),
            ],
        ),
        out_shape=jax.ShapeDtypeStruct((side, side, 48, 1536), bf16),
        compiler_params=pltpu.CompilerParams(vmem_limit_bytes=40 << 20),
        cost_estimate=pl.CostEstimate(
            flops=2 * 768 * 1536 * 1536, bytes_accessed=12 << 20, transcendentals=0
        ),
    )(at, *chunks, in_own, in_par, out_own, out_par)


def grad_kernel(at, a_own, a_oth, b_own, b_oth, gin_ref, gout_ref):
    core = at[0]
    first = (((0,), (0,)), ((), ()))

    def both(x, g, act, hid):
        gout_ref[...] = lax.dot_general(act[...], g[...], first, preferred_element_type=f32).astype(
            bf16
        )
        gin_ref[...] = lax.dot_general(x[...], hid[...], first, preferred_element_type=f32).astype(
            bf16
        )

    pl.when(core == 0)(lambda: both(a_own, a_oth, b_own, b_oth))
    pl.when(core == 1)(lambda: both(a_oth, a_own, b_oth, b_own))


def weight_grads(at, a_own, a_oth, b_own, b_oth):
    part = pl.BlockSpec((768, tile), lambda j, at: (0, j))
    whole = pl.BlockSpec((768, 768), lambda j, at: (0, 0))
    return pl.pallas_call(
        grad_kernel,
        grid_spec=pltpu.PrefetchScalarGridSpec(
            num_scalar_prefetch=1,
            grid=(6,),
            in_specs=[part, part, whole, whole],
            out_specs=[
                pl.BlockSpec((tile, 768), lambda j, at: (j, 0)),
                pl.BlockSpec((768, tile), lambda j, at: (0, j)),
            ],
        ),
        out_shape=[
            jax.ShapeDtypeStruct((1536, 768), bf16),
            jax.ShapeDtypeStruct((768, 1536), bf16),
        ],
        compiler_params=pltpu.CompilerParams(vmem_limit_bytes=40 << 20),
        cost_estimate=pl.CostEstimate(
            flops=4 * 768 * 768 * 1536, bytes_accessed=12 << 20, transcendentals=0
        ),
    )(at, a_own, a_oth, b_own, b_oth)


def local(inputs, w_in, w_out, out_grad):
    core = lax.axis_index("row") % 2
    me = lax.axis_index("col")
    at = jnp.stack([core, me]).astype(jnp.int32)
    fore = core == 0

    got = swap_cores(jnp.where(fore, out_grad, inputs))
    mine = jnp.where(fore, inputs, out_grad)
    pair = jnp.concatenate([jnp.where(fore, mine, got), jnp.where(fore, got, mine)])
    row = [pair] + [first_axis(pair, by) for by in steps]
    row = jnp.concatenate(row)
    blocks = [row] + [second_axis(row, by) for by in steps]
    in_par = swap_cores(w_in)
    out_par = swap_cores(w_out)

    sums, gathered = first_product(at, blocks, w_in, in_par, w_out, out_par)
    sums = sums.reshape(ring, 96, 1536)

    up, down = sums[4, :, :768], sums[4, :, 768:]
    for left in (3, 2, 1, 0):
        up, down = decoded(along_z(coded(up), 1)), decoded(along_z(coded(down), -1))
        if left == 3:
            up = jnp.pad(up, ((0, 0), (0, 768)))
            down = jnp.pad(down, ((0, 0), (768, 0)))
        if left:
            up, down = sums[left] + up, sums[ring - left] + down
    total = sums[0] + up + down
    gathered = gathered.reshape(768, 1536)
    total, gathered, gathered_oth = lax.optimization_barrier(
        (total, gathered, swap_cores(gathered))
    )

    other = swap_cores(total)
    value, slopes = gelu_parts(jnp.where(fore, total, other))
    hid = jnp.where(fore, other, total) * slopes
    here = jnp.where(fore, value, hid).astype(bf16)

    chunks = [here] + [None] * (ring - 1)
    up = down = here
    for far in (1, 2, 3):
        up, down = along_z(up, 1), along_z(down, -1)
        chunks[ring - far], chunks[far] = up, down
    chunks[4] = jnp.concatenate([along_z(up[:, :768], 1), along_z(down[:, 768:], -1)], axis=1)

    acts = jnp.concatenate(chunks)
    acts_own = jnp.where(fore, acts[:, :768], acts[:, 768:])
    acts_oth = swap_cores(jnp.where(fore, acts[:, 768:], acts[:, :768]))
    partial = second_product(at, chunks, w_in, in_par, w_out, out_par)
    partial, acts_oth = lax.optimization_barrier((partial, acts_oth))

    kept = partial[0].astype(f32)
    for k, by in enumerate(steps):
        kept = kept + second_axis(partial[k + 1], -by).astype(f32)
    grad_in, grad_out = weight_grads(at, gathered, gathered_oth, acts_own, acts_oth)
    kept, grad_in, grad_out = lax.optimization_barrier((kept, grad_in, grad_out))
    last = kept[0]
    for k, by in enumerate(steps):
        last = last + first_axis(kept[k + 1].astype(bf16), -by).astype(f32)
    last = last.astype(bf16)
    keep = jnp.where(fore, last[:24], last[24:])
    came = swap_cores(jnp.where(fore, last[24:], last[:24]))
    output = jnp.where(fore, keep, came)
    input_grad = jnp.where(fore, came, keep)
    return (output, input_grad, grad_in, grad_out)


def solution(mesh):
    placed = (P("row", "col"), P("col", "row"), P("row", "col"), P("row", "col"))
    return jax.shard_map(
        local,
        mesh=mesh,
        in_specs=placed,
        out_specs=(P("row", "col"), P("row", "col"), P("col", "row"), P("row", "col")),
        check_vma=False,
    )
```

```python
import jax
import jax.numpy as jnp
from jax import lax
from jax.experimental import pallas as pl
from jax.experimental.pallas import tpu as pltpu
from jax.sharding import PartitionSpec as P

gelu_scale = 0.7978845608028654
gelu_cubic = 0.044715
f32 = jnp.float32
bf16 = jnp.bfloat16
side = 4
ring = 8
tile = 256
steps = (1, -1, 2)
barrier = lax.optimization_barrier


def gelu_parts(hidden):
    inner = gelu_scale * (hidden + gelu_cubic * hidden * hidden * hidden)
    tangent = jnp.tanh(inner)
    value = 0.5 * hidden * (1.0 + tangent)
    slopes = 0.5 * (1.0 + tangent) + 0.5 * hidden * (1.0 - tangent * tangent) * gelu_scale * (
        1.0 + 3.0 * gelu_cubic * hidden * hidden
    )
    return (value, slopes)


def coded(array):
    array = array * 2.0**30
    return (array * array * array).astype(bf16)


def decoded(array):
    array = array.astype(f32)
    return jnp.sign(array) * jnp.exp2(jnp.log2(jnp.abs(array)) * (1.0 / 3.0) - 30.0)


def place(x, y, core):
    return ((x % side) * side + y % side) * 2 + core


def swap_cores(array):
    return lax.ppermute(array, "row", [(r, r ^ 1) for r in range(32)])


def first_axis(array, by):
    pairs = []
    for x in range(side):
        for y in range(side):
            pairs.append((place(x, y, 0), place(x + by, y, 0)))
            pairs.append((place(x, y, 1), place(x, y + by, 1)))
    return lax.ppermute(array, "row", pairs)


def second_axis(array, by):
    pairs = []
    for x in range(side):
        for y in range(side):
            pairs.append((place(x, y, 0), place(x, y + by, 0)))
            pairs.append((place(x, y, 1), place(x + by, y, 1)))
    return lax.ppermute(array, "row", pairs)


def along_z(array, by):
    return lax.ppermute(array, "col", [(z, (z + by) % ring) for z in range(ring)])


def slot(at, outer, inner):
    core, me = at[0], at[1]
    spot = jnp.where(core == 0, inner * side + outer, outer * side + inner)
    return lax.rem(spot // 2 + ring - me, ring), lax.rem(spot, 2)


def call(kernel, at, args, in_specs, out_specs, out_shape, grid, macs, scratch=()):
    return pl.pallas_call(
        kernel,
        grid_spec=pltpu.PrefetchScalarGridSpec(
            num_scalar_prefetch=1,
            grid=grid,
            in_specs=in_specs,
            out_specs=out_specs,
            scratch_shapes=scratch,
        ),
        out_shape=out_shape,
        compiler_params=pltpu.CompilerParams(vmem_limit_bytes=32 << 20),
        cost_estimate=pl.CostEstimate(
            flops=2 * macs, bytes_accessed=8 << 20, transcendentals=0
        ),
    )(at, *args)


def shape(*dims, of=bf16):
    return jax.ShapeDtypeStruct(dims, of)


def fixed(*dims):
    return pl.BlockSpec(dims, lambda j, at: (0,) * len(dims))


def pair_kernel(at, mine, got, out):
    a, b = mine[...].astype(f32), got[...].astype(f32)
    core = at[0]

    @pl.when(core == 0)
    def _():
        out[...] = jnp.concatenate([a, b]).astype(bf16)

    @pl.when(core == 1)
    def _():
        out[...] = jnp.concatenate([b, a]).astype(bf16)


def make_pair(at, mine, got):
    return call(
        pair_kernel, at, (mine, got), [fixed(24, 1536)] * 2, fixed(48, 1536), shape(48, 1536), (1,), 0
    )


def turn_kernel(at, in_own, in_par, out_own, out_par, one_own, one_par, two_own, two_par):
    core = at[0]

    @pl.when(core == 0)
    def _():
        one_own[...] = in_own[...]
        one_par[...] = in_par[...]
        two_own[...] = out_own[...]
        two_par[...] = out_par[...]

    @pl.when(core == 1)
    def _():
        one_own[...] = out_own[...].T
        one_par[...] = out_par[...].T
        two_own[...] = in_own[...].T
        two_par[...] = in_par[...].T


def turned(at, in_own, in_par, out_own, out_par):
    tall = pl.BlockSpec((1536, tile), lambda j, at: (0, j))
    wide = pl.BlockSpec((tile, 1536), lambda j, at: (j, 0))
    return call(
        turn_kernel,
        at,
        (in_own, in_par, out_own, out_par),
        [tall, tall, wide, wide],
        [tall, tall, wide, wide],
        [shape(1536, 768)] * 2 + [shape(768, 1536)] * 2,
        (3,),
        0,
    )


halves = [
    pl.BlockSpec((1536, tile), lambda j, at: (0, jnp.minimum(j, 2))),
    pl.BlockSpec((1536, tile), lambda j, at: (0, jnp.maximum(j - 3, 0))),
]


def farthest_kernel(at, own, par, a0, a1, a2, a3, all_ref, up_ref, down_ref):
    step = pl.program_id(0)

    @pl.when(step == 0)
    def _():
        for outer, ref in enumerate((a0, a1, a2, a3)):
            for inner in range(side):
                chunk, half = slot(at, outer, inner)
                all_ref[chunk, half] = ref[pl.ds(inner * 48, 48), :]

    def product(w):
        a = all_ref[4].reshape(96, 1536)
        return jnp.dot(a, w[...], preferred_element_type=f32).astype(bf16)

    @pl.when(step < 3)
    def _():
        up_ref[...] = product(own)

    @pl.when(step >= 3)
    def _():
        down_ref[...] = product(par)


def farthest(at, own, par, blocks):
    return call(
        farthest_kernel,
        at,
        (own, par, *blocks),
        halves + [fixed(192, 1536)] * 4,
        [
            fixed(ring, 2, 48, 1536),
            pl.BlockSpec((96, tile), lambda j, at: (0, jnp.minimum(j, 2))),
            pl.BlockSpec((96, tile), lambda j, at: (0, jnp.maximum(j - 3, 0))),
        ],
        [shape(ring, 2, 48, 1536), shape(96, 768), shape(96, 768)],
        (6,),
        96 * 1536 * 1536,
    )


def first_product(at, own, par, gathered, picked):
    n = len(picked)

    def kernel(at, own, par, *refs):
        step = pl.program_id(0)

        def product(w):
            a = jnp.concatenate([ref[0].reshape(96, 1536) for ref in refs[:n]])
            h = jnp.dot(a, w[...], preferred_element_type=f32)
            for i, out in enumerate(refs[n:]):
                out[...] = h[i * 96 : (i + 1) * 96]

        pl.when(step < 3)(lambda: product(own))
        pl.when(step >= 3)(lambda: product(par))

    def chunk(i):
        return pl.BlockSpec((1, 2, 48, 1536), lambda j, at: (i, 0, 0, 0))

    return call(
        kernel,
        at,
        (own, par) + (gathered,) * n,
        halves + [chunk(i) for i in picked],
        [pl.BlockSpec((96, tile), lambda j, at: (0, j))] * n,
        [shape(96, 1536, of=f32)] * n,
        (6,),
        n * 96 * 1536 * 1536,
    )


columns = [pl.BlockSpec((768, tile), lambda j, at: (0, j))] * 2
wide_tile = pl.BlockSpec((96, tile), lambda j, at: (0, j))


def second_product(at, own, par, chunks):
    n = len(chunks)

    def kernel(at, own, par, *refs):
        b = jnp.concatenate([ref[...] for ref in refs[:n]])
        o = jnp.dot(b[:, :768], own[...], preferred_element_type=f32) + jnp.dot(
            b[:, 768:], par[...], preferred_element_type=f32
        )
        for i, out in enumerate(refs[n:]):
            out[...] = o[i * 96 : (i + 1) * 96].astype(bf16)

    return call(
        kernel,
        at,
        (own, par, *chunks),
        columns + [fixed(96, 1536)] * n,
        [wide_tile] * n,
        [shape(96, 1536)] * n,
        (6,),
        n * 96 * 1536 * 1536,
    )


def last_kernel(at, own, par, b_own, b_par, *refs):
    ready, (o_ref, made) = refs[: ring - 1], refs[ring - 1 :]
    o = jnp.dot(b_own[...], own[...], preferred_element_type=f32) + jnp.dot(
        b_par[...], par[...], preferred_element_type=f32
    )
    spare = iter(ready)
    for i in range(ring):
        part = o.astype(bf16) if i == 4 else next(spare)[...]
        made[i] = part.reshape(2, 48, tile)
    for outer in range(side):
        for inner in range(side):
            chunk, half = slot(at, outer, inner)
            o_ref[outer, inner] = made[chunk, half]


def last_product(at, own, par, b_own, b_par, ready):
    return call(
        last_kernel,
        at,
        (own, par, b_own, b_par, *ready),
        columns + [fixed(96, 768)] * 2 + [wide_tile] * (ring - 1),
        pl.BlockSpec((side, side, 48, tile), lambda j, at: (0, 0, 0, j)),
        shape(side, side, 48, 1536),
        (6,),
        96 * 1536 * 1536,
        scratch=[pltpu.VMEM((ring, 2, 48, tile), bf16)],
    )


def grad_kernel(at, a_own, a_oth, b_own, b_oth, gin_ref, gout_ref):
    core = at[0]
    first = (((0,), (0,)), ((), ()))

    def both(x, g, act, hid):
        gout_ref[...] = lax.dot_general(act[...], g[...], first, preferred_element_type=f32).astype(
            bf16
        )
        gin_ref[...] = lax.dot_general(x[...], hid[...], first, preferred_element_type=f32).astype(
            bf16
        )

    pl.when(core == 0)(lambda: both(a_own, a_oth, b_own, b_oth))
    pl.when(core == 1)(lambda: both(a_oth, a_own, b_oth, b_own))


def weight_grads(at, a_own, a_oth, b_own, b_oth):
    part = pl.BlockSpec((768, tile), lambda j, at: (0, j))
    return call(
        grad_kernel,
        at,
        (a_own, a_oth, b_own, b_oth),
        [part, part, fixed(768, 768), fixed(768, 768)],
        [pl.BlockSpec((tile, 768), lambda j, at: (j, 0)), part],
        [shape(1536, 768), shape(768, 1536)],
        (6,),
        2 * 768 * 768 * 1536,
    )


def local(inputs, w_in, w_out, out_grad):
    core = lax.axis_index("row") % 2
    me = lax.axis_index("col")
    at = jnp.stack([core, me]).astype(jnp.int32)
    fore = core == 0

    mine = jnp.where(fore, inputs, out_grad)
    got = swap_cores(jnp.where(fore, out_grad, inputs))
    got, send_in, send_out = barrier((got, w_in, w_out))
    in_par, out_par = swap_cores(send_in), swap_cores(send_out)
    pair = make_pair(at, mine, got)
    row = jnp.concatenate([pair] + [first_axis(pair, by) for by in steps])
    row, late = barrier((row, at))
    blocks = [row] + [second_axis(row, by) for by in steps]
    one, par_one, two, par_two = turned(late, w_in, in_par, w_out, out_par)
    *blocks, one, par_one = barrier((*blocks, one, par_one))

    gathered, up, down = farthest(at, one, par_one, blocks)
    for left in (3, 2, 1):
        came_up, came_down = along_z(up, 1), along_z(down, -1)
        picked = (left, ring - left) if left > 1 else (1, ring - 1, 0)
        parts = first_product(at, one, par_one, gathered, picked)
        came_up, came_down, *parts = barrier((came_up, came_down, *parts))
        if left < 2:
            came_up, came_down = decoded(came_up), decoded(came_down)
        came_up, came_down = came_up.astype(f32), came_down.astype(f32)
        if left == 3:
            came_up = jnp.pad(came_up, ((0, 0), (0, 768)))
            came_down = jnp.pad(came_down, ((0, 0), (768, 0)))
            gathered_oth = swap_cores(gathered)
        up, down = parts[0] + came_up, parts[1] + came_down
        up, down = (up.astype(bf16), down.astype(bf16)) if left > 2 else (coded(up), coded(down))
        up, down, gathered = barrier((up, down, gathered))
    total = parts[2] + decoded(along_z(up, 1)) + decoded(along_z(down, -1))
    total, gathered, gathered_oth = barrier((total, gathered, gathered_oth))

    other = swap_cores(total)
    other = jnp.concatenate([other[:, 768:], other[:, :768]], axis=1)
    value, slopes = gelu_parts(jnp.where(fore, total, other))
    hid = jnp.where(fore, other, total) * slopes
    here = jnp.where(fore, value, hid).astype(bf16)

    chunks, ready = {0: here}, {}
    up = down = here
    for far in (1, 2, 3, 4):
        came_up, came_down = (up, down) if far < 4 else (up[:, :768], down[:, 768:])
        came_up, came_down = along_z(came_up, 1), along_z(came_down, -1)
        names = [0] if far == 1 else [far - 1, ring + 1 - far]
        made = second_product(at, two, par_two, [chunks[i] for i in names])
        ready.update(zip(names, made))
        up, down, *made = barrier((came_up, came_down, *made))
        ready.update(zip(names, made))
        if far < 4:
            chunks[ring - far], chunks[far] = up, down
    order = [0, 1, 2, 3, 5, 6, 7]
    acts_own = [chunks[i][:, :768] for i in order]
    acts_own = jnp.concatenate(acts_own[:4] + [up] + acts_own[4:])
    acts_oth = [chunks[i][:, 768:] for i in order]
    acts_oth = swap_cores(jnp.concatenate(acts_oth[:4] + [down] + acts_oth[4:]))
    partial = last_product(at, two, par_two, up, down, [ready[i] for i in order])
    partial, acts_oth = barrier((partial, acts_oth))

    kept = partial[0].astype(f32)
    for k, by in enumerate(steps):
        kept = kept + second_axis(partial[k + 1], -by).astype(f32)
    gathered, gathered_oth = gathered.reshape(768, 1536), gathered_oth.reshape(768, 1536)
    grad_in, grad_out = weight_grads(at, gathered, gathered_oth, acts_own, acts_oth)
    kept, grad_in, grad_out = barrier((kept, grad_in, grad_out))
    last = kept[0]
    for k, by in enumerate(steps):
        last = last + first_axis(kept[k + 1].astype(bf16), -by).astype(f32)
    last = last.astype(bf16)
    keep = jnp.where(fore, last[:24], last[24:])
    came = swap_cores(jnp.where(fore, last[24:], last[:24]))
    output = jnp.where(fore, keep, came)
    input_grad = jnp.where(fore, came, keep)
    return (output, input_grad, grad_in, grad_out)


def solution(mesh):
    placed = (P("row", "col"), P("col", "row"), P("row", "col"), P("row", "col"))
    return jax.shard_map(
        local,
        mesh=mesh,
        in_specs=placed,
        out_specs=(P("row", "col"), P("row", "col"), P("col", "row"), P("row", "col")),
        check_vma=False,
    )
```

```python
import jax
import jax.numpy as jnp
from jax import lax
from jax.experimental import pallas as pl
from jax.experimental.pallas import tpu as pltpu
from jax.sharding import PartitionSpec as P

gelu_scale = 0.7978845608028654
gelu_cubic = 0.044715
f32 = jnp.float32
bf16 = jnp.bfloat16
side = 4
ring = 8
tile = 256
steps = (2, 1, -1)
barrier = lax.optimization_barrier


def gelu_parts(hidden):
    inner = gelu_scale * (hidden + gelu_cubic * hidden * hidden * hidden)
    tangent = jnp.tanh(inner)
    value = 0.5 * hidden * (1.0 + tangent)
    slopes = 0.5 * (1.0 + tangent) + 0.5 * hidden * (1.0 - tangent * tangent) * gelu_scale * (
        1.0 + 3.0 * gelu_cubic * hidden * hidden
    )
    return (value, slopes)


def coded(array):
    array = array * 2.0**30
    return (array * array * array).astype(bf16)


def decoded(array):
    array = array.astype(f32)
    return jnp.sign(array) * jnp.exp2(jnp.log2(jnp.abs(array)) * (1.0 / 3.0) - 30.0)


def place(x, y, core):
    return ((x % side) * side + y % side) * 2 + core


def swap_cores(array):
    return lax.ppermute(array, "row", [(r, r ^ 1) for r in range(32)])


def first_axis(array, by):
    pairs = []
    for x in range(side):
        for y in range(side):
            pairs.append((place(x, y, 0), place(x + by, y, 0)))
            pairs.append((place(x, y, 1), place(x, y + by, 1)))
    return lax.ppermute(array, "row", pairs)


def second_axis(array, by):
    pairs = []
    for x in range(side):
        for y in range(side):
            pairs.append((place(x, y, 0), place(x, y + by, 0)))
            pairs.append((place(x, y, 1), place(x + by, y, 1)))
    return lax.ppermute(array, "row", pairs)


def along_z(array, by):
    return lax.ppermute(array, "col", [(z, (z + by) % ring) for z in range(ring)])


def slot(at, outer, inner):
    core, me = at[0], at[1]
    spot = jnp.where(core == 0, inner * side + outer, outer * side + inner)
    return lax.rem(spot // 2 + ring - me, ring), lax.rem(spot, 2)


def call(kernel, at, args, in_specs, out_specs, out_shape, grid, macs, scratch=()):
    return pl.pallas_call(
        kernel,
        grid_spec=pltpu.PrefetchScalarGridSpec(
            num_scalar_prefetch=1,
            grid=grid,
            in_specs=in_specs,
            out_specs=out_specs,
            scratch_shapes=scratch,
        ),
        out_shape=out_shape,
        compiler_params=pltpu.CompilerParams(vmem_limit_bytes=32 << 20),
        cost_estimate=pl.CostEstimate(
            flops=2 * macs, bytes_accessed=8 << 20, transcendentals=0
        ),
    )(at, *args)


def shape(*dims, of=bf16):
    return jax.ShapeDtypeStruct(dims, of)


def fixed(*dims):
    return pl.BlockSpec(dims, lambda j, at: (0,) * len(dims))


def pair_kernel(at, mine, got, out):
    a, b = mine[...].astype(f32), got[...].astype(f32)
    core = at[0]

    @pl.when(core == 0)
    def _():
        out[...] = jnp.concatenate([a, b]).astype(bf16)

    @pl.when(core == 1)
    def _():
        out[...] = jnp.concatenate([b, a]).astype(bf16)


def make_pair(at, mine, got):
    return call(
        pair_kernel, at, (mine, got), [fixed(24, 1536)] * 2, fixed(48, 1536), shape(48, 1536), (1,), 0
    )


def turn_kernel(at, in_own, in_par, out_own, out_par, one_own, one_par, two_own, two_par):
    core = at[0]

    @pl.when(core == 0)
    def _():
        one_own[...] = in_own[...]
        one_par[...] = in_par[...]
        two_own[...] = out_own[...]
        two_par[...] = out_par[...]

    @pl.when(core == 1)
    def _():
        one_own[...] = out_own[...].T
        one_par[...] = out_par[...].T
        two_own[...] = in_own[...].T
        two_par[...] = in_par[...].T


def turned(at, in_own, in_par, out_own, out_par):
    tall = pl.BlockSpec((1536, tile), lambda j, at: (0, j))
    wide = pl.BlockSpec((tile, 1536), lambda j, at: (j, 0))
    return call(
        turn_kernel,
        at,
        (in_own, in_par, out_own, out_par),
        [tall, tall, wide, wide],
        [tall, tall, wide, wide],
        [shape(1536, 768)] * 2 + [shape(768, 1536)] * 2,
        (3,),
        0,
    )


halves = [
    pl.BlockSpec((1536, tile), lambda j, at: (0, jnp.minimum(j, 2))),
    pl.BlockSpec((1536, tile), lambda j, at: (0, jnp.maximum(j - 3, 0))),
]


def farthest_kernel(at, own, par, a0, a1, a2, a3, all_ref, up_ref, down_ref):
    step = pl.program_id(0)

    @pl.when(step == 0)
    def _():
        for outer, ref in enumerate((a0, a1, a2, a3)):
            for inner in range(side):
                chunk, half = slot(at, outer, inner)
                all_ref[chunk, half] = ref[pl.ds(inner * 48, 48), :]

    def product(w):
        a = all_ref[4].reshape(96, 1536)
        return jnp.dot(a, w[...], preferred_element_type=f32).astype(bf16)

    @pl.when(step < 3)
    def _():
        up_ref[...] = product(own)

    @pl.when(step >= 3)
    def _():
        down_ref[...] = product(par)


def farthest(at, own, par, blocks):
    return call(
        farthest_kernel,
        at,
        (own, par, *blocks),
        halves + [fixed(192, 1536)] * 4,
        [
            fixed(ring, 2, 48, 1536),
            pl.BlockSpec((96, tile), lambda j, at: (0, jnp.minimum(j, 2))),
            pl.BlockSpec((96, tile), lambda j, at: (0, jnp.maximum(j - 3, 0))),
        ],
        [shape(ring, 2, 48, 1536), shape(96, 768), shape(96, 768)],
        (6,),
        96 * 1536 * 1536,
    )


def first_product(at, own, par, gathered, picked):
    n = len(picked)

    def kernel(at, own, par, *refs):
        step = pl.program_id(0)

        def product(w):
            a = jnp.concatenate([ref[0].reshape(96, 1536) for ref in refs[:n]])
            h = jnp.dot(a, w[...], preferred_element_type=f32)
            for i, out in enumerate(refs[n:]):
                out[...] = h[i * 96 : (i + 1) * 96]

        pl.when(step < 3)(lambda: product(own))
        pl.when(step >= 3)(lambda: product(par))

    def chunk(i):
        return pl.BlockSpec((1, 2, 48, 1536), lambda j, at: (i, 0, 0, 0))

    return call(
        kernel,
        at,
        (own, par) + (gathered,) * n,
        halves + [chunk(i) for i in picked],
        [pl.BlockSpec((96, tile), lambda j, at: (0, j))] * n,
        [shape(96, 1536, of=f32)] * n,
        (6,),
        n * 96 * 1536 * 1536,
    )


columns = [pl.BlockSpec((768, tile), lambda j, at: (0, j))] * 2
wide_tile = pl.BlockSpec((96, tile), lambda j, at: (0, j))


def second_product(at, own, par, chunks):
    n = len(chunks)

    def kernel(at, own, par, *refs):
        b = jnp.concatenate([ref[...] for ref in refs[:n]])
        o = jnp.dot(b[:, :768], own[...], preferred_element_type=f32) + jnp.dot(
            b[:, 768:], par[...], preferred_element_type=f32
        )
        for i, out in enumerate(refs[n:]):
            out[...] = o[i * 96 : (i + 1) * 96].astype(bf16)

    return call(
        kernel,
        at,
        (own, par, *chunks),
        columns + [fixed(96, 1536)] * n,
        [wide_tile] * n,
        [shape(96, 1536)] * n,
        (6,),
        n * 96 * 1536 * 1536,
    )


def last_kernel(at, own, par, b_own, b_par, *refs):
    ready, (o_ref, made) = refs[: ring - 1], refs[ring - 1 :]
    o = jnp.dot(b_own[...], own[...], preferred_element_type=f32) + jnp.dot(
        b_par[...], par[...], preferred_element_type=f32
    )
    spare = iter(ready)
    for i in range(ring):
        part = o.astype(bf16) if i == 4 else next(spare)[...]
        made[i] = part.reshape(2, 48, tile)
    for outer in range(side):
        for inner in range(side):
            chunk, half = slot(at, outer, inner)
            o_ref[outer, inner] = made[chunk, half]


def last_product(at, own, par, b_own, b_par, ready):
    return call(
        last_kernel,
        at,
        (own, par, b_own, b_par, *ready),
        columns + [fixed(96, 768)] * 2 + [wide_tile] * (ring - 1),
        pl.BlockSpec((side, side, 48, tile), lambda j, at: (0, 0, 0, j)),
        shape(side, side, 48, 1536),
        (6,),
        96 * 1536 * 1536,
        scratch=[pltpu.VMEM((ring, 2, 48, tile), bf16)],
    )


def grad_kernel(at, a_own, a_oth, b_own, b_oth, gin_ref, gout_ref):
    core = at[0]
    first = (((0,), (0,)), ((), ()))

    def both(x, g, act, hid):
        gout_ref[...] = lax.dot_general(act[...], g[...], first, preferred_element_type=f32).astype(
            bf16
        )
        gin_ref[...] = lax.dot_general(x[...], hid[...], first, preferred_element_type=f32).astype(
            bf16
        )

    pl.when(core == 0)(lambda: both(a_own, a_oth, b_own, b_oth))
    pl.when(core == 1)(lambda: both(a_oth, a_own, b_oth, b_own))


def weight_grads(at, a_own, a_oth, b_own, b_oth):
    part = pl.BlockSpec((768, tile), lambda j, at: (0, j))
    return call(
        grad_kernel,
        at,
        (a_own, a_oth, b_own, b_oth),
        [part, part, fixed(768, 768), fixed(768, 768)],
        [pl.BlockSpec((tile, 768), lambda j, at: (j, 0)), part],
        [shape(1536, 768), shape(768, 1536)],
        (6,),
        2 * 768 * 768 * 1536,
    )


def local(inputs, w_in, w_out, out_grad):
    core = lax.axis_index("row") % 2
    me = lax.axis_index("col")
    at = jnp.stack([core, me]).astype(jnp.int32)
    fore = core == 0

    mine = jnp.where(fore, inputs, out_grad)
    got = swap_cores(jnp.where(fore, out_grad, inputs))
    got, send_in, send_out = barrier((got, w_in, w_out))
    in_par, out_par = swap_cores(send_in), swap_cores(send_out)
    pair = make_pair(at, mine, got)
    row = jnp.concatenate([pair] + [first_axis(pair, by) for by in steps])
    row, late = barrier((row, at))
    blocks = [row] + [second_axis(row, by) for by in steps]
    one, par_one, two, par_two = turned(late, w_in, in_par, w_out, out_par)
    *blocks, one, par_one = barrier((*blocks, one, par_one))

    gathered, up, down = farthest(at, one, par_one, blocks)
    for left in (3, 2, 1):
        came_up, came_down = along_z(up, 1), along_z(down, -1)
        picked = (left, ring - left) if left > 1 else (1, ring - 1, 0)
        parts = first_product(at, one, par_one, gathered, picked)
        came_up, came_down, *parts = barrier((came_up, came_down, *parts))
        if left < 2:
            came_up, came_down = decoded(came_up), decoded(came_down)
        came_up, came_down = came_up.astype(f32), came_down.astype(f32)
        if left == 3:
            came_up = jnp.pad(came_up, ((0, 0), (0, 768)))
            came_down = jnp.pad(came_down, ((0, 0), (768, 0)))
            gathered_oth = swap_cores(gathered)
        up, down = parts[0] + came_up, parts[1] + came_down
        up, down = (up.astype(bf16), down.astype(bf16)) if left > 2 else (coded(up), coded(down))
        up, down, gathered = barrier((up, down, gathered))
    total = parts[2] + decoded(along_z(up, 1)) + decoded(along_z(down, -1))
    total, gathered, gathered_oth = barrier((total, gathered, gathered_oth))

    other = swap_cores(total)
    other = jnp.concatenate([other[:, 768:], other[:, :768]], axis=1)
    value, slopes = gelu_parts(jnp.where(fore, total, other))
    hid = jnp.where(fore, other, total) * slopes
    here = jnp.where(fore, value, hid).astype(bf16)

    chunks, ready = {0: here}, {}
    up = down = here
    for far in (1, 2, 3, 4):
        came_up, came_down = (up, down) if far < 4 else (up[:, :768], down[:, 768:])
        came_up, came_down = along_z(came_up, 1), along_z(came_down, -1)
        names = [0] if far == 1 else [far - 1, ring + 1 - far]
        made = second_product(at, two, par_two, [chunks[i] for i in names])
        ready.update(zip(names, made))
        up, down, *made = barrier((came_up, came_down, *made))
        ready.update(zip(names, made))
        if far < 4:
            chunks[ring - far], chunks[far] = up, down
    order = [0, 1, 2, 3, 5, 6, 7]
    acts_own = [chunks[i][:, :768] for i in order]
    acts_own = jnp.concatenate(acts_own[:4] + [up] + acts_own[4:])
    acts_oth = [chunks[i][:, 768:] for i in order]
    acts_oth = swap_cores(jnp.concatenate(acts_oth[:4] + [down] + acts_oth[4:]))
    partial = last_product(at, two, par_two, up, down, [ready[i] for i in order])
    partial, acts_oth = barrier((partial, acts_oth))

    kept = partial[0].astype(f32)
    for k, by in enumerate(steps):
        kept = kept + second_axis(partial[k + 1], -by).astype(f32)
    gathered, gathered_oth = gathered.reshape(768, 1536), gathered_oth.reshape(768, 1536)
    grad_in, grad_out = weight_grads(at, gathered, gathered_oth, acts_own, acts_oth)
    kept, grad_in, grad_out = barrier((kept, grad_in, grad_out))
    last = kept[0]
    for k, by in enumerate(steps):
        last = last + first_axis(kept[k + 1].astype(bf16), -by).astype(f32)
    last = last.astype(bf16)
    keep = jnp.where(fore, last[:24], last[24:])
    came = swap_cores(jnp.where(fore, last[24:], last[:24]))
    output = jnp.where(fore, keep, came)
    input_grad = jnp.where(fore, came, keep)
    return (output, input_grad, grad_in, grad_out)


def solution(mesh):
    placed = (P("row", "col"), P("col", "row"), P("row", "col"), P("row", "col"))
    return jax.shard_map(
        local,
        mesh=mesh,
        in_specs=placed,
        out_specs=(P("row", "col"), P("row", "col"), P("col", "row"), P("row", "col")),
        check_vma=False,
    )
```

```python
import jax
import jax.numpy as jnp
from jax import lax
from jax.experimental import pallas as pl
from jax.experimental.pallas import tpu as pltpu
from jax.sharding import PartitionSpec as P

gelu_scale = 0.7978845608028654
gelu_cubic = 0.044715
f32 = jnp.float32
bf16 = jnp.bfloat16
side = 4
ring = 8
tile = 256
steps = (1, -1, 2)
barrier = lax.optimization_barrier


def gelu_parts(hidden):
    inner = gelu_scale * (hidden + gelu_cubic * hidden * hidden * hidden)
    tangent = jnp.tanh(inner)
    value = 0.5 * hidden * (1.0 + tangent)
    slopes = 0.5 * (1.0 + tangent) + 0.5 * hidden * (1.0 - tangent * tangent) * gelu_scale * (
        1.0 + 3.0 * gelu_cubic * hidden * hidden
    )
    return (value, slopes)


def coded(array):
    array = array * 2.0**30
    return (array * array * array).astype(bf16)


def decoded(array):
    array = array.astype(f32)
    return jnp.sign(array) * jnp.exp2(jnp.log2(jnp.abs(array)) * (1.0 / 3.0) - 30.0)


def place(x, y, core):
    return ((x % side) * side + y % side) * 2 + core


def swap_cores(array):
    return lax.ppermute(array, "row", [(r, r ^ 1) for r in range(32)])


def first_axis(array, by):
    pairs = []
    for x in range(side):
        for y in range(side):
            pairs.append((place(x, y, 0), place(x + by, y, 0)))
            pairs.append((place(x, y, 1), place(x, y + by, 1)))
    return lax.ppermute(array, "row", pairs)


def second_axis(array, by):
    pairs = []
    for x in range(side):
        for y in range(side):
            pairs.append((place(x, y, 0), place(x, y + by, 0)))
            pairs.append((place(x, y, 1), place(x + by, y, 1)))
    return lax.ppermute(array, "row", pairs)


def along_z(array, by):
    return lax.ppermute(array, "col", [(z, (z + by) % ring) for z in range(ring)])


def slot(at, outer, inner):
    core, me = at[0], at[1]
    spot = jnp.where(core == 0, inner * side + outer, outer * side + inner)
    return lax.rem(spot // 2 + ring - me, ring), lax.rem(spot, 2)


def call(kernel, at, args, in_specs, out_specs, out_shape, grid, macs, scratch=()):
    return pl.pallas_call(
        kernel,
        grid_spec=pltpu.PrefetchScalarGridSpec(
            num_scalar_prefetch=1,
            grid=grid,
            in_specs=in_specs,
            out_specs=out_specs,
            scratch_shapes=scratch,
        ),
        out_shape=out_shape,
        compiler_params=pltpu.CompilerParams(vmem_limit_bytes=32 << 20),
        cost_estimate=pl.CostEstimate(
            flops=2 * macs, bytes_accessed=8 << 20, transcendentals=0
        ),
    )(at, *args)


def shape(*dims, of=bf16):
    return jax.ShapeDtypeStruct(dims, of)


def fixed(*dims):
    return pl.BlockSpec(dims, lambda j, at: (0,) * len(dims))


def pair_kernel(at, mine, got, out):
    a, b = mine[...].astype(f32), got[...].astype(f32)
    core = at[0]

    @pl.when(core == 0)
    def _():
        out[...] = jnp.concatenate([a, b]).astype(bf16)

    @pl.when(core == 1)
    def _():
        out[...] = jnp.concatenate([b, a]).astype(bf16)


def make_pair(at, mine, got):
    return call(
        pair_kernel, at, (mine, got), [fixed(24, 1536)] * 2, fixed(48, 1536), shape(48, 1536), (1,), 0
    )


def turn_kernel(at, in_own, in_par, out_own, out_par, one_own, one_par, two_own, two_par):
    core = at[0]

    @pl.when(core == 0)
    def _():
        one_own[...] = in_own[...]
        one_par[...] = in_par[...]
        two_own[...] = out_own[...]
        two_par[...] = out_par[...]

    @pl.when(core == 1)
    def _():
        one_own[...] = out_own[...].T
        one_par[...] = out_par[...].T
        two_own[...] = in_own[...].T
        two_par[...] = in_par[...].T


def turned(at, in_own, in_par, out_own, out_par):
    tall = pl.BlockSpec((1536, tile), lambda j, at: (0, j))
    wide = pl.BlockSpec((tile, 1536), lambda j, at: (j, 0))
    return call(
        turn_kernel,
        at,
        (in_own, in_par, out_own, out_par),
        [tall, tall, wide, wide],
        [tall, tall, wide, wide],
        [shape(1536, 768)] * 2 + [shape(768, 1536)] * 2,
        (3,),
        0,
    )


halves = [
    pl.BlockSpec((1536, tile), lambda j, at: (0, jnp.minimum(j, 2))),
    pl.BlockSpec((1536, tile), lambda j, at: (0, jnp.maximum(j - 3, 0))),
]


def farthest_kernel(at, own, par, a0, a1, a2, a3, all_ref, up_ref, down_ref):
    step = pl.program_id(0)

    @pl.when(step == 0)
    def _():
        for outer, ref in enumerate((a0, a1, a2, a3)):
            for inner in range(side):
                chunk, half = slot(at, outer, inner)
                all_ref[chunk, half] = ref[pl.ds(inner * 48, 48), :]

    def product(w):
        a = all_ref[4].reshape(96, 1536)
        return jnp.dot(a, w[...], preferred_element_type=f32).astype(bf16)

    @pl.when(step < 3)
    def _():
        up_ref[...] = product(own)

    @pl.when(step >= 3)
    def _():
        down_ref[...] = product(par)


def farthest(at, own, par, blocks):
    return call(
        farthest_kernel,
        at,
        (own, par, *blocks),
        halves + [fixed(192, 1536)] * 4,
        [
            fixed(ring, 2, 48, 1536),
            pl.BlockSpec((96, tile), lambda j, at: (0, jnp.minimum(j, 2))),
            pl.BlockSpec((96, tile), lambda j, at: (0, jnp.maximum(j - 3, 0))),
        ],
        [shape(ring, 2, 48, 1536), shape(96, 768), shape(96, 768)],
        (6,),
        96 * 1536 * 1536,
    )


def first_product(at, own, par, gathered, picked):
    n = len(picked)

    def kernel(at, own, par, *refs):
        step = pl.program_id(0)

        def product(w):
            a = jnp.concatenate([ref[0].reshape(96, 1536) for ref in refs[:n]])
            h = jnp.dot(a, w[...], preferred_element_type=f32)
            for i, out in enumerate(refs[n:]):
                out[...] = h[i * 96 : (i + 1) * 96]

        pl.when(step < 3)(lambda: product(own))
        pl.when(step >= 3)(lambda: product(par))

    def chunk(i):
        return pl.BlockSpec((1, 2, 48, 1536), lambda j, at: (i, 0, 0, 0))

    return call(
        kernel,
        at,
        (own, par) + (gathered,) * n,
        halves + [chunk(i) for i in picked],
        [pl.BlockSpec((96, tile), lambda j, at: (0, j))] * n,
        [shape(96, 1536, of=f32)] * n,
        (6,),
        n * 96 * 1536 * 1536,
    )


columns = [pl.BlockSpec((768, tile), lambda j, at: (0, j))] * 2
wide_tile = pl.BlockSpec((96, tile), lambda j, at: (0, j))


def second_product(at, own, par, chunks):
    n = len(chunks)

    def kernel(at, own, par, *refs):
        b = jnp.concatenate([ref[...] for ref in refs[:n]])
        o = jnp.dot(b[:, :768], own[...], preferred_element_type=f32) + jnp.dot(
            b[:, 768:], par[...], preferred_element_type=f32
        )
        for i, out in enumerate(refs[n:]):
            out[...] = o[i * 96 : (i + 1) * 96].astype(bf16)

    return call(
        kernel,
        at,
        (own, par, *chunks),
        columns + [fixed(96, 1536)] * n,
        [wide_tile] * n,
        [shape(96, 1536)] * n,
        (6,),
        n * 96 * 1536 * 1536,
    )


def last_kernel(at, own, par, b_own, b_par, *refs):
    ready, (o_ref, made) = refs[: ring - 1], refs[ring - 1 :]
    o = jnp.dot(b_own[...], own[...], preferred_element_type=f32) + jnp.dot(
        b_par[...], par[...], preferred_element_type=f32
    )
    spare = iter(ready)
    for i in range(ring):
        part = o.astype(bf16) if i == 4 else next(spare)[...]
        made[i] = part.reshape(2, 48, tile)
    for outer in range(side):
        for inner in range(side):
            chunk, half = slot(at, outer, inner)
            o_ref[outer, inner] = made[chunk, half]


def last_product(at, own, par, b_own, b_par, ready):
    return call(
        last_kernel,
        at,
        (own, par, b_own, b_par, *ready),
        columns + [fixed(96, 768)] * 2 + [wide_tile] * (ring - 1),
        pl.BlockSpec((side, side, 48, tile), lambda j, at: (0, 0, 0, j)),
        shape(side, side, 48, 1536),
        (6,),
        96 * 1536 * 1536,
        scratch=[pltpu.VMEM((ring, 2, 48, tile), bf16)],
    )


def grad_kernel(at, a_own, a_oth, b_own, b_oth, gin_ref, gout_ref):
    core = at[0]
    first = (((0,), (0,)), ((), ()))

    def both(x, g, act, hid):
        gout_ref[...] = lax.dot_general(act[...], g[...], first, preferred_element_type=f32).astype(
            bf16
        )
        gin_ref[...] = lax.dot_general(x[...], hid[...], first, preferred_element_type=f32).astype(
            bf16
        )

    pl.when(core == 0)(lambda: both(a_own, a_oth, b_own, b_oth))
    pl.when(core == 1)(lambda: both(a_oth, a_own, b_oth, b_own))


def weight_grads(at, a_own, a_oth, b_own, b_oth):
    part = pl.BlockSpec((768, tile), lambda j, at: (0, j))
    return call(
        grad_kernel,
        at,
        (a_own, a_oth, b_own, b_oth),
        [part, part, fixed(768, 768), fixed(768, 768)],
        [pl.BlockSpec((tile, 768), lambda j, at: (j, 0)), part],
        [shape(1536, 768), shape(768, 1536)],
        (6,),
        2 * 768 * 768 * 1536,
    )


def local(inputs, w_in, w_out, out_grad):
    core = lax.axis_index("row") % 2
    me = lax.axis_index("col")
    at = jnp.stack([core, me]).astype(jnp.int32)
    fore = core == 0

    mine = jnp.where(fore, inputs, out_grad)
    got = swap_cores(jnp.where(fore, out_grad, inputs))
    got, send_in, send_out = barrier((got, w_in, w_out))
    in_par, out_par = swap_cores(send_in), swap_cores(send_out)
    pair = make_pair(at, mine, got)
    row = jnp.concatenate([pair] + [first_axis(pair, by) for by in steps])
    row, late = barrier((row, at))
    far = second_axis(row, steps[2])
    blocks = [row] + [second_axis(row, by) for by in steps[:2]] + [far]
    one, par_one, two, par_two = turned(late, w_in, in_par, w_out, out_par)
    *blocks, one, par_one = barrier((*blocks, one, par_one))

    gathered, up, down = farthest(at, one, par_one, blocks)
    for left in (3, 2, 1):
        came_up, came_down = along_z(up, 1), along_z(down, -1)
        picked = (left, ring - left) if left > 1 else (1, ring - 1, 0)
        parts = first_product(at, one, par_one, gathered, picked)
        came_up, came_down, *parts = barrier((came_up, came_down, *parts))
        if left < 2:
            came_up, came_down = decoded(came_up), decoded(came_down)
        came_up, came_down = came_up.astype(f32), came_down.astype(f32)
        if left == 3:
            came_up = jnp.pad(came_up, ((0, 0), (0, 768)))
            came_down = jnp.pad(came_down, ((0, 0), (768, 0)))
            gathered_oth = swap_cores(gathered)
        up, down = parts[0] + came_up, parts[1] + came_down
        up, down = (up.astype(bf16), down.astype(bf16)) if left > 2 else (coded(up), coded(down))
        up, down, gathered = barrier((up, down, gathered))
    total = parts[2] + decoded(along_z(up, 1)) + decoded(along_z(down, -1))
    total, gathered, gathered_oth = barrier((total, gathered, gathered_oth))

    other = swap_cores(total)
    other = jnp.concatenate([other[:, 768:], other[:, :768]], axis=1)
    value, slopes = gelu_parts(jnp.where(fore, total, other))
    hid = jnp.where(fore, other, total) * slopes
    here = jnp.where(fore, value, hid).astype(bf16)

    chunks, ready = {0: here}, {}
    up = down = here
    for far in (1, 2, 3, 4):
        came_up, came_down = (up, down) if far < 4 else (up[:, :768], down[:, 768:])
        came_up, came_down = along_z(came_up, 1), along_z(came_down, -1)
        names = [0] if far == 1 else [far - 1, ring + 1 - far]
        made = second_product(at, two, par_two, [chunks[i] for i in names])
        ready.update(zip(names, made))
        up, down, *made = barrier((came_up, came_down, *made))
        ready.update(zip(names, made))
        if far < 4:
            chunks[ring - far], chunks[far] = up, down
    order = [0, 1, 2, 3, 5, 6, 7]
    acts_own = [chunks[i][:, :768] for i in order]
    acts_own = jnp.concatenate(acts_own[:4] + [up] + acts_own[4:])
    acts_oth = [chunks[i][:, 768:] for i in order]
    acts_oth = swap_cores(jnp.concatenate(acts_oth[:4] + [down] + acts_oth[4:]))
    partial = last_product(at, two, par_two, up, down, [ready[i] for i in order])
    partial, acts_oth = barrier((partial, acts_oth))

    kept = partial[0].astype(f32)
    for k, by in enumerate(steps):
        kept = kept + second_axis(partial[k + 1], -by).astype(f32)
    gathered, gathered_oth = gathered.reshape(768, 1536), gathered_oth.reshape(768, 1536)
    grad_in, grad_out = weight_grads(at, gathered, gathered_oth, acts_own, acts_oth)
    kept, grad_in, grad_out = barrier((kept, grad_in, grad_out))
    last = kept[0]
    for k, by in enumerate(steps):
        last = last + first_axis(kept[k + 1].astype(bf16), -by).astype(f32)
    last = last.astype(bf16)
    keep = jnp.where(fore, last[:24], last[24:])
    came = swap_cores(jnp.where(fore, last[24:], last[:24]))
    output = jnp.where(fore, keep, came)
    input_grad = jnp.where(fore, came, keep)
    return (output, input_grad, grad_in, grad_out)


def solution(mesh):
    placed = (P("row", "col"), P("col", "row"), P("row", "col"), P("row", "col"))
    return jax.shard_map(
        local,
        mesh=mesh,
        in_specs=placed,
        out_specs=(P("row", "col"), P("row", "col"), P("col", "row"), P("row", "col")),
        check_vma=False,
    )
```

```python
import jax
import jax.numpy as jnp
from jax import lax
from jax.experimental import pallas as pl
from jax.experimental.pallas import tpu as pltpu
from jax.sharding import PartitionSpec as P

gelu_scale = 0.7978845608028654
gelu_cubic = 0.044715
f32 = jnp.float32
bf16 = jnp.bfloat16
side = 4
ring = 8
tile = 256
steps = (1, -1, 2)
barrier = lax.optimization_barrier


def gelu_parts(hidden):
    inner = gelu_scale * (hidden + gelu_cubic * hidden * hidden * hidden)
    tangent = jnp.tanh(inner)
    value = 0.5 * hidden * (1.0 + tangent)
    slopes = 0.5 * (1.0 + tangent) + 0.5 * hidden * (1.0 - tangent * tangent) * gelu_scale * (
        1.0 + 3.0 * gelu_cubic * hidden * hidden
    )
    return (value, slopes)


def coded(array):
    array = array * 2.0**30
    return (array * array * array).astype(bf16)


def decoded(array):
    array = array.astype(f32)
    return jnp.sign(array) * jnp.exp2(jnp.log2(jnp.abs(array)) * (1.0 / 3.0) - 30.0)


def place(x, y, core):
    return ((x % side) * side + y % side) * 2 + core


def swap_cores(array):
    return lax.ppermute(array, "row", [(r, r ^ 1) for r in range(32)])


def first_axis(array, by):
    pairs = []
    for x in range(side):
        for y in range(side):
            pairs.append((place(x, y, 0), place(x + by, y, 0)))
            pairs.append((place(x, y, 1), place(x, y + by, 1)))
    return lax.ppermute(array, "row", pairs)


def second_axis(array, by):
    pairs = []
    for x in range(side):
        for y in range(side):
            pairs.append((place(x, y, 0), place(x, y + by, 0)))
            pairs.append((place(x, y, 1), place(x + by, y, 1)))
    return lax.ppermute(array, "row", pairs)


def along_z(array, by):
    return lax.ppermute(array, "col", [(z, (z + by) % ring) for z in range(ring)])


def slot(at, outer, inner):
    core, me = at[0], at[1]
    spot = jnp.where(core == 0, inner * side + outer, outer * side + inner)
    return lax.rem(spot // 2 + ring - me, ring), lax.rem(spot, 2)


def call(kernel, at, args, in_specs, out_specs, out_shape, grid, macs, scratch=()):
    return pl.pallas_call(
        kernel,
        grid_spec=pltpu.PrefetchScalarGridSpec(
            num_scalar_prefetch=1,
            grid=grid,
            in_specs=in_specs,
            out_specs=out_specs,
            scratch_shapes=scratch,
        ),
        out_shape=out_shape,
        compiler_params=pltpu.CompilerParams(vmem_limit_bytes=32 << 20),
        cost_estimate=pl.CostEstimate(
            flops=2 * macs, bytes_accessed=8 << 20, transcendentals=0
        ),
    )(at, *args)


def shape(*dims, of=bf16):
    return jax.ShapeDtypeStruct(dims, of)


def fixed(*dims):
    return pl.BlockSpec(dims, lambda j, at: (0,) * len(dims))


def pair_kernel(at, inputs, out_grad, got_in, got_grad, out):
    core = at[0]

    def join(a, b):
        out[...] = jnp.concatenate([a[...].astype(f32), b[...].astype(f32)]).astype(bf16)

    pl.when(core == 0)(lambda: join(inputs, got_in))
    pl.when(core == 1)(lambda: join(got_grad, out_grad))


def make_pair(at, *parts):
    return call(
        pair_kernel, at, parts, [fixed(24, 1536)] * 4, fixed(48, 1536), shape(48, 1536), (1,), 0
    )


def turn_kernel(at, in_own, in_par, out_own, out_par, one_own, one_par, two_own, two_par):
    core = at[0]

    @pl.when(core == 0)
    def _():
        one_own[...] = in_own[...]
        one_par[...] = in_par[...]
        two_own[...] = out_own[...]
        two_par[...] = out_par[...]

    @pl.when(core == 1)
    def _():
        one_own[...] = out_own[...].T
        one_par[...] = out_par[...].T
        two_own[...] = in_own[...].T
        two_par[...] = in_par[...].T


def turned(at, in_own, in_par, out_own, out_par):
    tall = pl.BlockSpec((1536, tile), lambda j, at: (0, j))
    wide = pl.BlockSpec((tile, 1536), lambda j, at: (j, 0))
    return call(
        turn_kernel,
        at,
        (in_own, in_par, out_own, out_par),
        [tall, tall, wide, wide],
        [tall, tall, wide, wide],
        [shape(1536, 768)] * 2 + [shape(768, 1536)] * 2,
        (3,),
        0,
    )


halves = [
    pl.BlockSpec((1536, tile), lambda j, at: (0, jnp.minimum(j, 2))),
    pl.BlockSpec((1536, tile), lambda j, at: (0, jnp.maximum(j - 3, 0))),
]


def farthest_kernel(at, own, par, a0, a1, a2, a3, all_ref, up_ref, down_ref):
    step = pl.program_id(0)

    @pl.when(step == 0)
    def _():
        for outer, ref in enumerate((a0, a1, a2, a3)):
            for inner in range(side):
                chunk, half = slot(at, outer, inner)
                all_ref[chunk, half] = ref[pl.ds(inner * 48, 48), :]

    def product(w):
        a = all_ref[4].reshape(96, 1536)
        return jnp.dot(a, w[...], preferred_element_type=f32).astype(bf16)

    @pl.when(step < 3)
    def _():
        up_ref[...] = product(own)

    @pl.when(step >= 3)
    def _():
        down_ref[...] = product(par)


def farthest(at, own, par, blocks):
    return call(
        farthest_kernel,
        at,
        (own, par, *blocks),
        halves + [fixed(192, 1536)] * 4,
        [
            fixed(ring, 2, 48, 1536),
            pl.BlockSpec((96, tile), lambda j, at: (0, jnp.minimum(j, 2))),
            pl.BlockSpec((96, tile), lambda j, at: (0, jnp.maximum(j - 3, 0))),
        ],
        [shape(ring, 2, 48, 1536), shape(96, 768), shape(96, 768)],
        (6,),
        96 * 1536 * 1536,
    )


def first_product(at, own, par, gathered, picked):
    n = len(picked)

    def kernel(at, own, par, *refs):
        step = pl.program_id(0)

        def product(w):
            a = jnp.concatenate([ref[0].reshape(96, 1536) for ref in refs[:n]])
            h = jnp.dot(a, w[...], preferred_element_type=f32)
            for i, out in enumerate(refs[n:]):
                out[...] = h[i * 96 : (i + 1) * 96]

        pl.when(step < 3)(lambda: product(own))
        pl.when(step >= 3)(lambda: product(par))

    def chunk(i):
        return pl.BlockSpec((1, 2, 48, 1536), lambda j, at: (i, 0, 0, 0))

    return call(
        kernel,
        at,
        (own, par) + (gathered,) * n,
        halves + [chunk(i) for i in picked],
        [pl.BlockSpec((96, tile), lambda j, at: (0, j))] * n,
        [shape(96, 1536, of=f32)] * n,
        (6,),
        n * 96 * 1536 * 1536,
    )


columns = [pl.BlockSpec((768, tile), lambda j, at: (0, j))] * 2
wide_tile = pl.BlockSpec((96, tile), lambda j, at: (0, j))


def second_product(at, own, par, chunks):
    n = len(chunks)

    def kernel(at, own, par, *refs):
        b = jnp.concatenate([ref[...] for ref in refs[:n]])
        o = jnp.dot(b[:, :768], own[...], preferred_element_type=f32) + jnp.dot(
            b[:, 768:], par[...], preferred_element_type=f32
        )
        for i, out in enumerate(refs[n:]):
            out[...] = o[i * 96 : (i + 1) * 96].astype(bf16)

    return call(
        kernel,
        at,
        (own, par, *chunks),
        columns + [fixed(96, 1536)] * n,
        [wide_tile] * n,
        [shape(96, 1536)] * n,
        (6,),
        n * 96 * 1536 * 1536,
    )


def last_kernel(at, own, par, b_own, b_par, *refs):
    ready, (o_ref, made) = refs[: ring - 1], refs[ring - 1 :]
    o = jnp.dot(b_own[...], own[...], preferred_element_type=f32) + jnp.dot(
        b_par[...], par[...], preferred_element_type=f32
    )
    spare = iter(ready)
    for i in range(ring):
        part = o.astype(bf16) if i == 4 else next(spare)[...]
        made[i] = part.reshape(2, 48, tile)
    for outer in range(side):
        for inner in range(side):
            chunk, half = slot(at, outer, inner)
            o_ref[outer, inner] = made[chunk, half]


def last_product(at, own, par, b_own, b_par, ready):
    return call(
        last_kernel,
        at,
        (own, par, b_own, b_par, *ready),
        columns + [fixed(96, 768)] * 2 + [wide_tile] * (ring - 1),
        pl.BlockSpec((side, side, 48, tile), lambda j, at: (0, 0, 0, j)),
        shape(side, side, 48, 1536),
        (6,),
        96 * 1536 * 1536,
        scratch=[pltpu.VMEM((ring, 2, 48, tile), bf16)],
    )


def grad_kernel(at, a_own, a_oth, b_own, b_oth, gin_ref, gout_ref):
    core = at[0]
    first = (((0,), (0,)), ((), ()))

    def both(x, g, act, hid):
        gout_ref[...] = lax.dot_general(act[...], g[...], first, preferred_element_type=f32).astype(
            bf16
        )
        gin_ref[...] = lax.dot_general(x[...], hid[...], first, preferred_element_type=f32).astype(
            bf16
        )

    pl.when(core == 0)(lambda: both(a_own, a_oth, b_own, b_oth))
    pl.when(core == 1)(lambda: both(a_oth, a_own, b_oth, b_own))


def weight_grads(at, a_own, a_oth, b_own, b_oth):
    part = pl.BlockSpec((768, tile), lambda j, at: (0, j))
    return call(
        grad_kernel,
        at,
        (a_own, a_oth, b_own, b_oth),
        [part, part, fixed(768, 768), fixed(768, 768)],
        [pl.BlockSpec((tile, 768), lambda j, at: (j, 0)), part],
        [shape(1536, 768), shape(768, 1536)],
        (6,),
        2 * 768 * 768 * 1536,
    )


def local(inputs, w_in, w_out, out_grad):
    core = lax.axis_index("row") % 2
    me = lax.axis_index("col")
    at = jnp.stack([core, me]).astype(jnp.int32)
    fore = core == 0

    got_in, got_grad = swap_cores(inputs), swap_cores(out_grad)
    got_in, got_grad, send_in, send_out = barrier((got_in, got_grad, w_in, w_out))
    in_par, out_par = swap_cores(send_in), swap_cores(send_out)
    pair = make_pair(at, inputs, out_grad, got_in, got_grad)
    row = jnp.concatenate([pair] + [first_axis(pair, by) for by in steps])
    row, late = barrier((row, at))
    blocks = [row] + [second_axis(row, by) for by in steps]
    one, par_one, two, par_two = turned(late, w_in, in_par, w_out, out_par)
    *blocks, one, par_one = barrier((*blocks, one, par_one))

    gathered, up, down = farthest(at, one, par_one, blocks)
    for left in (3, 2, 1):
        came_up, came_down = along_z(up, 1), along_z(down, -1)
        picked = (left, ring - left) if left > 1 else (1, ring - 1, 0)
        parts = first_product(at, one, par_one, gathered, picked)
        came_up, came_down, *parts = barrier((came_up, came_down, *parts))
        if left < 2:
            came_up, came_down = decoded(came_up), decoded(came_down)
        came_up, came_down = came_up.astype(f32), came_down.astype(f32)
        if left == 3:
            came_up = jnp.pad(came_up, ((0, 0), (0, 768)))
            came_down = jnp.pad(came_down, ((0, 0), (768, 0)))
            gathered_oth = swap_cores(gathered)
        up, down = parts[0] + came_up, parts[1] + came_down
        up, down = (up.astype(bf16), down.astype(bf16)) if left > 2 else (coded(up), coded(down))
        up, down, gathered = barrier((up, down, gathered))
    total = parts[2] + decoded(along_z(up, 1)) + decoded(along_z(down, -1))
    total, gathered, gathered_oth = barrier((total, gathered, gathered_oth))

    other = swap_cores(total)
    other = jnp.concatenate([other[:, 768:], other[:, :768]], axis=1)
    value, slopes = gelu_parts(jnp.where(fore, total, other))
    hid = jnp.where(fore, other, total) * slopes
    here = jnp.where(fore, value, hid).astype(bf16)

    chunks, ready = {0: here}, {}
    up = down = here
    for far in (1, 2, 3, 4):
        came_up, came_down = (up, down) if far < 4 else (up[:, :768], down[:, 768:])
        came_up, came_down = along_z(came_up, 1), along_z(came_down, -1)
        names = [0] if far == 1 else [far - 1, ring + 1 - far]
        made = second_product(at, two, par_two, [chunks[i] for i in names])
        ready.update(zip(names, made))
        up, down, *made = barrier((came_up, came_down, *made))
        ready.update(zip(names, made))
        if far < 4:
            chunks[ring - far], chunks[far] = up, down
    order = [0, 1, 2, 3, 5, 6, 7]
    acts_own = [chunks[i][:, :768] for i in order]
    acts_own = jnp.concatenate(acts_own[:4] + [up] + acts_own[4:])
    acts_oth = [chunks[i][:, 768:] for i in order]
    acts_oth = swap_cores(jnp.concatenate(acts_oth[:4] + [down] + acts_oth[4:]))
    partial = last_product(at, two, par_two, up, down, [ready[i] for i in order])
    partial, acts_oth = barrier((partial, acts_oth))

    kept = partial[0].astype(f32)
    for k, by in enumerate(steps):
        kept = kept + second_axis(partial[k + 1], -by).astype(f32)
    gathered, gathered_oth = gathered.reshape(768, 1536), gathered_oth.reshape(768, 1536)
    grad_in, grad_out = weight_grads(at, gathered, gathered_oth, acts_own, acts_oth)
    kept, grad_in, grad_out = barrier((kept, grad_in, grad_out))
    last = kept[0]
    for k, by in enumerate(steps):
        last = last + first_axis(kept[k + 1].astype(bf16), -by).astype(f32)
    last = last.astype(bf16)
    keep = jnp.where(fore, last[:24], last[24:])
    came = swap_cores(jnp.where(fore, last[24:], last[:24]))
    output = jnp.where(fore, keep, came)
    input_grad = jnp.where(fore, came, keep)
    return (output, input_grad, grad_in, grad_out)


def solution(mesh):
    placed = (P("row", "col"), P("col", "row"), P("row", "col"), P("row", "col"))
    return jax.shard_map(
        local,
        mesh=mesh,
        in_specs=placed,
        out_specs=(P("row", "col"), P("row", "col"), P("col", "row"), P("row", "col")),
        check_vma=False,
    )
```
